256 devices in a mesh: seq: 64 (over y, x_hi, z), grp: 4 (over x_lo, core).
Axes of the slice: x: 4 (x_hi: 2, x_lo: 2; x = x_hi * 2 + x_lo), y: 4, z: 8, core: 2. Of those that a mesh axis runs over, the one named last changes fastest.
Arguments:
- query_gate: bfloat16 [4, 8192, 2048], P('grp', 'seq'), may hold values from -6 to 6
- key_gate: bfloat16 [4, 8192, 2048], P('grp', 'seq'), may hold values from -6 to 6
- value_in: bfloat16 [4, 8192, 2048], P('grp', 'seq'), may hold values from -6 to 6
- grad_out: bfloat16 [4, 8192, 2048], P('grp', 'seq'), may hold values from -6 to 6
- filter_taps: float32 [8192, 2048], P('seq'), may hold values from -6 to 6
- skip_gain: float32 [2048], replicated, may hold values from 0.25 to 2
Outputs:
- query_grad: bfloat16 [4, 8192, 2048], P('grp', 'seq')
- key_grad: bfloat16 [4, 8192, 2048], P('grp', 'seq')
- value_grad: bfloat16 [4, 8192, 2048], P('grp', 'seq')
- filter_grad: float32 [8192, 2048], P('seq')
The draws below stay inside these ranges and needn't reach their ends.
All inputs are finite; a program needn't handle non-finite values.
Results may differ from the reference program's by a relative error of at most 0.001.
Values sent between devices are 32-bit elements; how exact they have to be, the bound alone decides.
No kernel may reach another device: no remote copies, remote signals or barrier semaphores. Data moves between devices by JAX's collectives and lax.ppermute only.
A program may use at most 128 MiB of HBM per device.

```python
import math
import jax
import jax.numpy as jnp

CH = 2048
SEQLEN = 8192
BATCH = 4


def level_of(own_key, dims, cuts, low, largest):
    level, own = 1.0, jax.random.fold_in(own_key, 6)
    for dim, parts in cuts:
        steps = jnp.exp(jax.random.uniform(jax.random.fold_in(own, dim), (parts,), jnp.float32, low / len(cuts), largest / len(cuts)))
        level = level * jnp.repeat(steps, dims[dim] // parts).reshape([-1 if axis == dim else 1 for axis in range(len(dims))])
    return level


def scatter_about(key, extent, scale, limit, pieces=(), dtype=jnp.bfloat16):
    factor_of = level_of(key, extent, pieces, -0.22, 0.18) if pieces else 1.0
    drawn = jax.random.normal(key, extent, jnp.float32) * scale * factor_of
    return jnp.minimum(jnp.maximum(drawn, -limit), limit).astype(dtype)


def setup_inputs(seed: int = 0) -> dict:
    keys = jax.random.split(jax.random.key(seed), 7)
    return {
        "query_gate": scatter_about(keys[0], (BATCH, SEQLEN, CH), 1.0, 6.0, ((0, 4), (1, 64))),
        "key_gate": scatter_about(keys[1], (BATCH, SEQLEN, CH), 1.0, 6.0, ((0, 4), (1, 64))),
        "value_in": scatter_about(keys[2], (BATCH, SEQLEN, CH), 1.0, 6.0, ((0, 4), (1, 64))),
        "grad_out": scatter_about(keys[3], (BATCH, SEQLEN, CH), 1.0, 6.0, ((0, 4), (1, 64))),
        "filter_taps": scatter_about(keys[4], (SEQLEN, CH), 1.0, 6.0, ((0, 64),), jnp.float32),
        "skip_gain": jnp.clip(jax.random.uniform(keys[5], (CH,), jnp.float32, 0.25, 2.0), 0.25, 2.0),
    }


def reference(query_gate, key_gate, value_in, grad_out, filter_taps, skip_gain):
    full_len = 2 * SEQLEN
    scale = 1.0 / math.sqrt(SEQLEN)
    filt_spec = jnp.fft.rfft(filter_taps, n=full_len, axis=0)
    query_list = []
    key_list = []
    value_list = []
    filter_total = jnp.zeros((SEQLEN, CH), jnp.float32)
    for member in range(BATCH):
        key_rows = key_gate[member].astype(jnp.float32)
        value_rows = value_in[member].astype(jnp.float32)
        grad_rows = grad_out[member].astype(jnp.float32)
        query_rows = query_gate[member].astype(jnp.float32)
        product = key_rows * value_rows
        gated_grad = query_rows * grad_rows
        prod_spec = jnp.fft.rfft(product, n=full_len, axis=0)
        grad_spec = jnp.fft.rfft(gated_grad, n=full_len, axis=0)
        conv_out = jnp.fft.irfft(prod_spec * filt_spec, n=full_len, axis=0)[:SEQLEN]
        back_conv = jnp.fft.irfft(grad_spec * jnp.conj(filt_spec), n=full_len, axis=0)[:SEQLEN]
        tap_term = jnp.fft.irfft(grad_spec * jnp.conj(prod_spec), n=full_len, axis=0)[:SEQLEN]
        mixed = scale * conv_out + skip_gain * product
        product_grad = scale * back_conv + skip_gain * gated_grad
        query_list.append((grad_rows * mixed).astype(jnp.bfloat16))
        key_list.append((product_grad * value_rows).astype(jnp.bfloat16))
        value_list.append((product_grad * key_rows).astype(jnp.bfloat16))
        filter_total = filter_total + tap_term.astype(jnp.float32)
    filter_grad = (scale * filter_total).astype(jnp.float32)
    return (jnp.stack(query_list), jnp.stack(key_list), jnp.stack(value_list), filter_grad)
```

```python
import functools
import math

import jax
import jax.numpy as jnp
import numpy as np
from jax import lax
from jax.experimental import pallas as pl
from jax.experimental.pallas import tpu as pltpu
from jax.sharding import PartitionSpec as P

f32 = jnp.float32
bf16 = jnp.bfloat16


def halves(table):
    high = np.asarray(table, np.float32).astype(jnp.bfloat16)
    low = (table - high.astype(np.float64)).astype(np.float32).astype(jnp.bfloat16)
    return high, low


def transform_tables(blocks, rows, scale):
    full = 2 * blocks * rows
    k1 = np.arange(blocks)[:, None] + 0.5
    first = 2.0 * math.pi * k1 * np.arange(blocks)[None, :] / (2 * blocks)
    twist = 2.0 * math.pi * k1 * np.arange(rows)[None, :] / full
    last = 2.0 * math.pi * np.arange(rows)[:, None] * np.arange(rows)[None, :] / rows
    c1, s1 = np.cos(first), np.sin(first)
    c2, s2 = np.cos(last), np.sin(last)
    ahead1 = halves(np.concatenate([c1, -s1], axis=0))
    ahead2 = halves(np.block([[c2, -s2], [s2, c2]]))
    back2 = halves(np.block([[c2, s2], [-s2, c2]]))
    back1 = halves(np.concatenate([c1.T, -s1.T], axis=1) * (2.0 * scale / full))
    stack1 = np.concatenate([ahead1[0], ahead1[1], ahead1[0]], axis=1)
    unstack1 = np.concatenate([back1[0], back1[1], back1[0]], axis=1)
    turn = np.stack([np.cos(twist), np.sin(twist)]).astype(np.float32)
    return stack1, turn, np.stack(ahead2), np.stack(back2), unstack1


def split(value):
    high = value.astype(bf16)
    return high, (value - high.astype(f32)).astype(bf16)


def dot(left, right):
    return jnp.dot(left, right, preferred_element_type=f32)


def dot3(value, table_ref):
    high, low = split(value)
    return dot(high, table_ref[0]) + dot(low, table_ref[0]) + dot(high, table_ref[1])


def pack_kernel(slots, query_ref, key_ref, value_ref, grad_ref, taps_ref, out_ref):
    rows, channels = query_ref.shape
    devices = channels // slots
    share = taps_ref.shape[1] // devices
    piece = 2 * slots + share
    per = devices // rows
    for block in range(channels // rows):
        slot, start = block // per, block % per * rows * piece
        cols = pl.ds(block * rows, rows)
        product = key_ref[:, cols].astype(f32) * value_ref[:, cols].astype(f32)
        gated = query_ref[:, cols].astype(f32) * grad_ref[:, cols].astype(f32)
        out_ref[pl.ds(start + slot, rows, stride=piece), :] = product.T
        out_ref[pl.ds(start + slots + slot, rows, stride=piece), :] = gated.T
    for block in range(share * per):
        slot, start = block // per, block % per * rows * piece
        taps = taps_ref[:, pl.ds(block * rows, rows)]
        out_ref[pl.ds(start + 2 * slots + slot, rows, stride=piece), :] = taps.T


def spectral_kernel(
    slots, groups, blocks, data_ref, first_ref, turn_ref, ahead_ref, back_ref, last_ref, out_ref
):
    share = slots // groups
    piece = 2 * slots + share
    rows = data_ref.shape[1]
    cos_t, sin_t = turn_ref[0], turn_ref[1]

    def rows_of(start):
        return pl.ds(start, blocks, stride=groups * piece)

    def forward(signals):
        high, low = split(jnp.concatenate(signals, axis=1))
        freq = dot(first_ref[...], jnp.concatenate([high, high, low], axis=0))
        turned = []
        for i in range(len(signals)):
            real = freq[:blocks, i * rows : (i + 1) * rows]
            imag = freq[blocks:, i * rows : (i + 1) * rows]
            turned.append(
                jnp.concatenate(
                    [real * cos_t + imag * sin_t, imag * cos_t - real * sin_t], axis=1
                )
            )
        spec = dot3(jnp.concatenate(turned, axis=0), ahead_ref)
        return [
            (spec[i * blocks : (i + 1) * blocks, :rows], spec[i * blocks : (i + 1) * blocks, rows:])
            for i in range(len(signals))
        ]

    def inverse(spectra):
        parts = dot3(
            jnp.concatenate([jnp.concatenate(pair, axis=1) for pair in spectra], axis=0), back_ref
        )
        turned = []
        for i in range(len(spectra)):
            real = parts[i * blocks : (i + 1) * blocks, :rows]
            imag = parts[i * blocks : (i + 1) * blocks, rows:]
            turned.append(
                jnp.concatenate(
                    [real * cos_t - imag * sin_t, imag * cos_t + real * sin_t], axis=0
                )
            )
        high, low = split(jnp.concatenate(turned, axis=1))
        out = dot(last_ref[...], jnp.concatenate([high, high, low], axis=0))
        return [out[:, i * rows : (i + 1) * rows] for i in range(len(spectra))]

    for slot in range(slots):
        tap_row = slot // share * piece + 2 * slots + slot % share
        starts = [tap_row]
        for group in range(groups):
            starts += [group * piece + slot, group * piece + slots + slot]
        spectra = forward([data_ref[rows_of(start), :] for start in starts])
        filt_r, filt_i = spectra[0]
        tap_r, tap_i = 0.0, 0.0
        products = []
        for group in range(groups):
            prod_r, prod_i = spectra[1 + 2 * group]
            grad_r, grad_i = spectra[2 + 2 * group]
            products.append((prod_r * filt_r - prod_i * filt_i, prod_r * filt_i + prod_i * filt_r))
            products.append((grad_r * filt_r + grad_i * filt_i, grad_i * filt_r - grad_r * filt_i))
            tap_r = tap_r + (grad_r * prod_r + grad_i * prod_i)
            tap_i = tap_i + (grad_i * prod_r - grad_r * prod_i)
        for start, value in zip(starts, inverse([(tap_r, tap_i)] + products)):
            out_ref[rows_of(start), :] = value


def gates_kernel(
    slots, query_ref, key_ref, value_ref, grad_ref, skip_ref, data_ref, dq_ref, dk_ref, dv_ref
):
    rows, channels = query_ref.shape
    devices = channels // slots
    piece = data_ref.shape[0] // devices
    per = devices // rows
    for block in range(channels // rows):
        slot, start = block // per, block % per * rows * piece
        cols = pl.ds(block * rows, rows)
        conv = data_ref[pl.ds(start + slot, rows, stride=piece), :].T
        back = data_ref[pl.ds(start + slots + slot, rows, stride=piece), :].T
        key = key_ref[:, cols].astype(f32)
        value = value_ref[:, cols].astype(f32)
        grad = grad_ref[:, cols].astype(f32)
        skip = skip_ref[:, cols]
        mixed = conv + skip * (key * value)
        product_grad = back + skip * (query_ref[:, cols].astype(f32) * grad)
        dq_ref[:, cols] = (grad * mixed).astype(bf16)
        dk_ref[:, cols] = (product_grad * value).astype(bf16)
        dv_ref[:, cols] = (product_grad * key).astype(bf16)


def own_taps_kernel(slots, devices, data_ref, out_ref):
    rows = out_ref.shape[0]
    piece = data_ref.shape[0] // devices
    per = devices // rows
    for block in range(out_ref.shape[1] // rows):
        slot, start = block // per, block % per * rows * piece
        out_ref[:, pl.ds(block * rows, rows)] = data_ref[
            pl.ds(start + 2 * slots + slot, rows, stride=piece), :
        ].T


def join_kernel(grp_ref, *refs):
    width = refs[0].shape[1]
    for step, ref in enumerate(refs[:-1]):
        start = pl.multiple_of((grp_ref[0] ^ step) * width, 128)
        refs[-1][:, pl.ds(start, width)] = ref[...]


def local_call(kernel, out_shape, n_in, flops, moved, scalar=False):
    vmem = pl.BlockSpec(memory_space=pltpu.VMEM)
    specs = [pl.BlockSpec(memory_space=pltpu.SMEM)] if scalar else []
    return pl.pallas_call(
        kernel,
        out_shape=out_shape,
        in_specs=specs + [vmem] * n_in,
        out_specs=jax.tree.map(lambda _: vmem, out_shape),
        compiler_params=pltpu.CompilerParams(vmem_limit_bytes=48 * 2**20),
        cost_estimate=pl.CostEstimate(flops=flops, bytes_accessed=moved, transcendentals=0),
    )


def exchange(pieces, devices):
    flat = pieces.reshape(devices, 1, pieces.shape[0] // devices * pieces.shape[1])
    moved = lax.all_to_all(flat, ("seq", "grp"), split_axis=0, concat_axis=0, tiled=True)
    return moved.reshape(pieces.shape)


def body(query_gate, key_gate, value_in, grad_out, filter_taps, skip_gain):
    rows, channels = filter_taps.shape
    blocks, groups = lax.axis_size("seq"), lax.axis_size("grp")
    devices = blocks * groups
    slots = channels // devices
    share = slots // groups
    piece = 2 * slots + share
    width = share * devices
    grp = lax.axis_index("grp")
    gates = (query_gate[0], key_gate[0], value_in[0], grad_out[0])
    own = lax.dynamic_slice_in_dim(filter_taps, grp * width, width, 1)
    pieces = jax.ShapeDtypeStruct((devices * piece, rows), f32)
    size = devices * piece * rows * 4
    sent = local_call(functools.partial(pack_kernel, slots), pieces, 5, 0, 2 * size)(*gates, own)
    data = exchange(sent, devices)
    tables = [
        jnp.asarray(table)
        for table in transform_tables(blocks, rows, 1.0 / math.sqrt(blocks * rows))
    ]
    result = local_call(
        functools.partial(spectral_kernel, slots, groups, blocks), pieces, 6, 5 * 10**9, 2 * size
    )(data, *tables)
    back = exchange(result, devices)
    own_grad = local_call(
        functools.partial(own_taps_kernel, slots, devices),
        jax.ShapeDtypeStruct((rows, width), f32),
        1,
        0,
        rows * width * 8,
    )(back)
    parts = [own_grad] + [
        lax.ppermute(own_grad, "grp", [(i, i ^ step) for i in range(groups)])
        for step in range(1, groups)
    ]
    grad_shape = jax.ShapeDtypeStruct((rows, channels), bf16)
    query_grad, key_grad, value_grad = local_call(
        functools.partial(gates_kernel, slots), [grad_shape] * 3, 6, 0, 20 * size
    )(*gates, skip_gain[None], back)
    filter_grad = local_call(
        join_kernel, jax.ShapeDtypeStruct((rows, channels), f32), groups, 0, 2 * size, scalar=True
    )(grp.reshape(1), *parts)
    return (query_grad[None], key_grad[None], value_grad[None], filter_grad)


def solution(mesh):
    split_rows = P("grp", "seq", None)
    return jax.shard_map(
        body,
        mesh=mesh,
        in_specs=(split_rows,) * 4 + (P("seq", None), P()),
        out_specs=(split_rows,) * 3 + (P("seq", None),),
        check_vma=False,
    )
```

```python
import functools
import math

import jax
import jax.numpy as jnp
import numpy as np
from jax import lax
from jax.experimental import pallas as pl
from jax.experimental.pallas import tpu as pltpu
from jax.sharding import PartitionSpec as P

f32 = jnp.float32
bf16 = jnp.bfloat16


def halves(table):
    high = np.asarray(table, np.float32).astype(jnp.bfloat16)
    low = (table - high.astype(np.float64)).astype(np.float32).astype(jnp.bfloat16)
    return high, low


def transform_tables(blocks, rows, scale):
    full = 2 * blocks * rows
    k1 = np.arange(blocks)[:, None] + 0.5
    first = 2.0 * math.pi * k1 * np.arange(blocks)[None, :] / (2 * blocks)
    twist = 2.0 * math.pi * k1 * np.arange(rows)[None, :] / full
    last = 2.0 * math.pi * np.arange(rows)[:, None] * np.arange(rows)[None, :] / rows
    c1, s1 = np.cos(first), np.sin(first)
    c2, s2 = np.cos(last), np.sin(last)
    ahead1 = halves(np.concatenate([c1, -s1], axis=0))
    ahead2 = halves(np.block([[c2, -s2], [s2, c2]]))
    back2 = halves(np.block([[c2, s2], [-s2, c2]]))
    back1 = halves(np.concatenate([c1.T, -s1.T], axis=1) * (2.0 * scale / full))
    stack1 = np.concatenate([ahead1[0], ahead1[1], ahead1[0]], axis=1)
    unstack1 = np.concatenate([back1[0], back1[1], back1[0]], axis=1)
    turn = np.stack([np.cos(twist), np.sin(twist)]).astype(np.float32)
    return stack1, turn, np.stack(ahead2), np.stack(back2), unstack1


def split(value):
    high = value.astype(bf16)
    return high, (value - high.astype(f32)).astype(bf16)


def dot(left, right):
    return jnp.dot(left, right, preferred_element_type=f32)


def dot3(value, table_ref):
    high, low = split(value)
    return dot(high, table_ref[0]) + dot(low, table_ref[0]) + dot(high, table_ref[1])


def pack_kernel(slots, parts, grp_ref, *refs):
    sources, taps_ref, out_ref, held, taps, sems, tap_sem = refs[:4], *refs[4:]
    rows, channels = sources[0].shape
    devices = channels // slots
    share = taps.shape[1] // devices
    piece = 2 * slots + share
    per = devices // rows
    width = channels // parts
    copies = []
    for part in range(parts):
        cols = pl.ds(part * width, width)
        copies.append(
            [
                pltpu.make_async_copy(ref.at[:, cols], held.at[i, :, cols], sems.at[i, part])
                for i, ref in enumerate(sources)
            ]
        )
        for copy in copies[-1]:
            copy.start()
    start = pl.multiple_of(grp_ref[0] * taps.shape[1], 128)
    tap_copy = pltpu.make_async_copy(taps_ref.at[:, pl.ds(start, taps.shape[1])], taps, tap_sem)
    tap_copy.start()
    for block in range(channels // rows):
        if block * rows % width == 0:
            for copy in copies[block * rows // width]:
                copy.wait()
        slot, start = block // per, block % per * rows * piece
        cols = pl.ds(block * rows, rows)
        query, key, value, grad = (held[i, :, cols].astype(f32) for i in range(4))
        out_ref[pl.ds(start + slot, rows, stride=piece), :] = (key * value).T
        out_ref[pl.ds(start + slots + slot, rows, stride=piece), :] = (query * grad).T
    tap_copy.wait()
    for block in range(share * per):
        slot, start = block // per, block % per * rows * piece
        own = taps[:, pl.ds(block * rows, rows)]
        out_ref[pl.ds(start + 2 * slots + slot, rows, stride=piece), :] = own.T


def spectral_kernel(
    slots, groups, blocks, data_ref, first_ref, turn_ref, ahead_ref, back_ref, last_ref, out_ref
):
    share = slots // groups
    piece = 2 * slots + share
    rows = data_ref.shape[1]
    cos_t, sin_t = turn_ref[0], turn_ref[1]

    def rows_of(start):
        return pl.ds(start, blocks, stride=groups * piece)

    def forward(signals):
        high, low = split(jnp.concatenate(signals, axis=1))
        freq = dot(first_ref[...], jnp.concatenate([high, high, low], axis=0))
        yield
        turned = []
        for i in range(len(signals)):
            real = freq[:blocks, i * rows : (i + 1) * rows]
            imag = freq[blocks:, i * rows : (i + 1) * rows]
            turned.append(
                jnp.concatenate(
                    [real * cos_t + imag * sin_t, imag * cos_t - real * sin_t], axis=1
                )
            )
        yield
        spec = dot3(jnp.concatenate(turned, axis=0), ahead_ref)
        yield [
            (spec[i * blocks : (i + 1) * blocks, :rows], spec[i * blocks : (i + 1) * blocks, rows:])
            for i in range(len(signals))
        ]

    def inverse(spectra):
        parts = dot3(
            jnp.concatenate([jnp.concatenate(pair, axis=1) for pair in spectra], axis=0), back_ref
        )
        yield
        turned = []
        for i in range(len(spectra)):
            real = parts[i * blocks : (i + 1) * blocks, :rows]
            imag = parts[i * blocks : (i + 1) * blocks, rows:]
            turned.append(
                jnp.concatenate(
                    [real * cos_t - imag * sin_t, imag * cos_t + real * sin_t], axis=0
                )
            )
        yield
        high, low = split(jnp.concatenate(turned, axis=1))
        out = dot(last_ref[...], jnp.concatenate([high, high, low], axis=0))
        yield [out[:, i * rows : (i + 1) * rows] for i in range(len(spectra))]

    def starts_of(slot):
        starts = [slot // share * piece + 2 * slots + slot % share]
        for group in range(groups):
            starts += [group * piece + slot, group * piece + slots + slot]
        return starts

    def products_of(spectra):
        filt_r, filt_i = spectra[0]
        tap_r, tap_i = 0.0, 0.0
        products = []
        for group in range(groups):
            prod_r, prod_i = spectra[1 + 2 * group]
            grad_r, grad_i = spectra[2 + 2 * group]
            products.append((prod_r * filt_r - prod_i * filt_i, prod_r * filt_i + prod_i * filt_r))
            products.append((grad_r * filt_r + grad_i * filt_i, grad_i * filt_r - grad_r * filt_i))
            tap_r = tap_r + (grad_r * prod_r + grad_i * prod_i)
            tap_i = tap_i + (grad_i * prod_r - grad_r * prod_i)
        return [(tap_r, tap_i)] + products

    before = None
    for slot in range(slots + 1):
        steps = []
        if slot < slots:
            steps.append(forward([data_ref[rows_of(start), :] for start in starts_of(slot)]))
        if before is not None:
            steps.append(inverse(before))
        for _ in range(2):
            for step in steps:
                next(step)
        results = [next(step) for step in steps]
        if before is not None:
            for start, value in zip(starts_of(slot - 1), results[-1]):
                out_ref[rows_of(start), :] = value
        before = products_of(results[0]) if slot < slots else None


def gates_kernel(
    slots, query_ref, key_ref, value_ref, grad_ref, skip_ref, data_ref, dq_ref, dk_ref, dv_ref
):
    rows, channels = query_ref.shape
    devices = channels // slots
    piece = data_ref.shape[0] // devices
    per = devices // rows
    for block in range(channels // rows):
        slot, start = block // per, block % per * rows * piece
        cols = pl.ds(block * rows, rows)
        conv = data_ref[pl.ds(start + slot, rows, stride=piece), :].T
        back = data_ref[pl.ds(start + slots + slot, rows, stride=piece), :].T
        key = key_ref[:, cols].astype(f32)
        value = value_ref[:, cols].astype(f32)
        grad = grad_ref[:, cols].astype(f32)
        skip = skip_ref[:, cols]
        mixed = conv + skip * (key * value)
        product_grad = back + skip * (query_ref[:, cols].astype(f32) * grad)
        dq_ref[:, cols] = (grad * mixed).astype(bf16)
        dk_ref[:, cols] = (product_grad * value).astype(bf16)
        dv_ref[:, cols] = (product_grad * key).astype(bf16)


def own_taps_kernel(slots, devices, data_ref, out_ref):
    rows = out_ref.shape[0]
    piece = data_ref.shape[0] // devices
    per = devices // rows
    for block in range(out_ref.shape[1] // rows):
        slot, start = block // per, block % per * rows * piece
        out_ref[:, pl.ds(block * rows, rows)] = data_ref[
            pl.ds(start + 2 * slots + slot, rows, stride=piece), :
        ].T


def join_kernel(grp_ref, *refs):
    width = refs[0].shape[1]
    for step, ref in enumerate(refs[:-1]):
        start = pl.multiple_of((grp_ref[0] ^ step) * width, 128)
        refs[-1][:, pl.ds(start, width)] = ref[...]


def local_call(kernel, out_shape, n_in, flops, moved, scalar=False):
    vmem = pl.BlockSpec(memory_space=pltpu.VMEM)
    specs = [pl.BlockSpec(memory_space=pltpu.SMEM)] if scalar else []
    return pl.pallas_call(
        kernel,
        out_shape=out_shape,
        in_specs=specs + [vmem] * n_in,
        out_specs=jax.tree.map(lambda _: vmem, out_shape),
        compiler_params=pltpu.CompilerParams(vmem_limit_bytes=48 * 2**20),
        cost_estimate=pl.CostEstimate(flops=flops, bytes_accessed=moved, transcendentals=0),
    )


def exchange(pieces, devices):
    flat = pieces.reshape(devices, 1, pieces.shape[0] // devices * pieces.shape[1])
    moved = lax.all_to_all(flat, ("seq", "grp"), split_axis=0, concat_axis=0, tiled=True)
    return moved.reshape(pieces.shape)


def body(query_gate, key_gate, value_in, grad_out, filter_taps, skip_gain):
    rows, channels = filter_taps.shape
    blocks, groups = lax.axis_size("seq"), lax.axis_size("grp")
    devices = blocks * groups
    slots = channels // devices
    share = slots // groups
    piece = 2 * slots + share
    width = share * devices
    grp = lax.axis_index("grp")
    gates = (query_gate[0], key_gate[0], value_in[0], grad_out[0])
    pieces = jax.ShapeDtypeStruct((devices * piece, rows), f32)
    size = devices * piece * rows * 4
    parts = 4
    sent = pl.pallas_call(
        functools.partial(pack_kernel, slots, parts),
        out_shape=pieces,
        in_specs=[pl.BlockSpec(memory_space=pltpu.SMEM)]
        + [pl.BlockSpec(memory_space=pltpu.HBM)] * 5,
        out_specs=pl.BlockSpec(memory_space=pltpu.VMEM),
        scratch_shapes=[
            pltpu.VMEM((4, rows, channels), bf16),
            pltpu.VMEM((rows, width), f32),
            pltpu.SemaphoreType.DMA((4, parts)),
            pltpu.SemaphoreType.DMA,
        ],
        compiler_params=pltpu.CompilerParams(vmem_limit_bytes=48 * 2**20),
        cost_estimate=pl.CostEstimate(flops=0, bytes_accessed=2 * size, transcendentals=0),
    )(
        grp.reshape(1),
        *(pltpu.with_memory_space_constraint(ref, pltpu.HBM) for ref in (*gates, filter_taps)),
    )
    data = exchange(sent, devices)
    tables = [
        jnp.asarray(table)
        for table in transform_tables(blocks, rows, 1.0 / math.sqrt(blocks * rows))
    ]
    result = local_call(
        functools.partial(spectral_kernel, slots, groups, blocks), pieces, 6, 5 * 10**9, 2 * size
    )(data, *tables)
    back = exchange(result, devices)
    own_grad = local_call(
        functools.partial(own_taps_kernel, slots, devices),
        jax.ShapeDtypeStruct((rows, width), f32),
        1,
        0,
        rows * width * 8,
    )(back)
    flip_core, flip_chip = ([(i, i ^ step) for i in range(groups)] for step in (1, 2))
    across = lax.ppermute(own_grad, "grp", flip_chip)
    beside = lax.ppermute(own_grad, "grp", flip_core)
    parts = [own_grad, beside, across, lax.ppermute(across, "grp", flip_core)]
    grad_shape = jax.ShapeDtypeStruct((rows, channels), bf16)
    query_grad, key_grad, value_grad = local_call(
        functools.partial(gates_kernel, slots), [grad_shape] * 3, 6, 0, 20 * size
    )(*gates, skip_gain[None], back)
    filter_grad = local_call(
        join_kernel, jax.ShapeDtypeStruct((rows, channels), f32), groups, 0, 2 * size, scalar=True
    )(grp.reshape(1), *parts)
    return (query_grad[None], key_grad[None], value_grad[None], filter_grad)


def solution(mesh):
    split_rows = P("grp", "seq", None)
    return jax.shard_map(
        body,
        mesh=mesh,
        in_specs=(split_rows,) * 4 + (P("seq", None), P()),
        out_specs=(split_rows,) * 3 + (P("seq", None),),
        check_vma=False,
    )
```

```python
import functools
import math

import jax
import jax.numpy as jnp
import numpy as np
from jax import lax
from jax.experimental import pallas as pl
from jax.experimental.pallas import tpu as pltpu
from jax.sharding import PartitionSpec as P

f32 = jnp.float32
bf16 = jnp.bfloat16


def halves(table):
    high = np.asarray(table, np.float32).astype(jnp.bfloat16)
    low = (table - high.astype(np.float64)).astype(np.float32).astype(jnp.bfloat16)
    return high, low


def transform_tables(blocks, rows, scale):
    full = 2 * blocks * rows
    k1 = np.arange(blocks)[:, None] + 0.5
    first = 2.0 * math.pi * k1 * np.arange(blocks)[None, :] / (2 * blocks)
    twist = 2.0 * math.pi * k1 * np.arange(rows)[None, :] / full
    last = 2.0 * math.pi * np.arange(rows)[:, None] * np.arange(rows)[None, :] / rows
    c1, s1 = np.cos(first), np.sin(first)
    c2, s2 = np.cos(last), np.sin(last)
    ahead1 = halves(np.concatenate([c1, -s1], axis=0))
    ahead2 = halves(np.block([[c2, -s2], [s2, c2]]))
    back2 = halves(np.block([[c2, s2], [-s2, c2]]))
    ahead2, back2 = (np.concatenate([h, h, l], axis=0) for h, l in (ahead2, back2))
    back1 = halves(np.concatenate([c1.T, -s1.T], axis=1) * (2.0 * scale / full))
    stack1 = np.concatenate([ahead1[0], ahead1[1], ahead1[0]], axis=1)
    unstack1 = np.concatenate([back1[0], back1[1], back1[0]], axis=1)
    turn = np.stack([np.cos(twist), np.sin(twist)]).astype(np.float32)
    return stack1, turn, ahead2, back2, unstack1


def split(value):
    high = value.astype(bf16)
    return high, (value - high.astype(f32)).astype(bf16)


def dot(left, right):
    return jnp.dot(left, right, preferred_element_type=f32)


def dot3(value, table_ref):
    high, low = split(value)
    return dot(jnp.concatenate([high, low, high], axis=1), table_ref[...])


def pack_kernel(slots, parts, grp_ref, *refs):
    sources, taps_ref, out_ref, held, taps, sems, tap_sem = refs[:4], *refs[4:]
    rows, channels = sources[0].shape
    devices = channels // slots
    share = taps.shape[1] // devices
    piece = 2 * slots + share
    per = devices // rows
    width = channels // parts
    copies = []
    for part in range(parts):
        cols = pl.ds(part * width, width)
        copies.append(
            [
                pltpu.make_async_copy(ref.at[:, cols], held.at[i, :, cols], sems.at[i, part])
                for i, ref in enumerate(sources)
            ]
        )
        for copy in copies[-1]:
            copy.start()
    start = pl.multiple_of(grp_ref[0] * taps.shape[1], 128)
    tap_copy = pltpu.make_async_copy(taps_ref.at[:, pl.ds(start, taps.shape[1])], taps, tap_sem)
    tap_copy.start()
    for block in range(channels // rows):
        if block * rows % width == 0:
            for copy in copies[block * rows // width]:
                copy.wait()
        slot, start = block // per, block % per * rows * piece
        cols = pl.ds(block * rows, rows)
        query, key, value, grad = (held[i, :, cols].astype(f32) for i in range(4))
        out_ref[pl.ds(start + slot, rows, stride=piece), :] = (key * value).T
        out_ref[pl.ds(start + slots + slot, rows, stride=piece), :] = (query * grad).T
    tap_copy.wait()
    for block in range(share * per):
        slot, start = block // per, block % per * rows * piece
        own = taps[:, pl.ds(block * rows, rows)]
        out_ref[pl.ds(start + 2 * slots + slot, rows, stride=piece), :] = own.T


def spectral_kernel(
    slots, groups, blocks, data_ref, first_ref, turn_ref, ahead_ref, back_ref, last_ref, out_ref
):
    share = slots // groups
    piece = 2 * slots + share
    rows = data_ref.shape[1]
    cos_t, sin_t = turn_ref[0], turn_ref[1]

    def rows_of(start):
        return pl.ds(start, blocks, stride=groups * piece)

    def forward(signals):
        high, low = split(jnp.concatenate(signals, axis=1))
        freq = dot(first_ref[...], jnp.concatenate([high, high, low], axis=0))
        yield
        turned = []
        for i in range(len(signals)):
            real = freq[:blocks, i * rows : (i + 1) * rows]
            imag = freq[blocks:, i * rows : (i + 1) * rows]
            turned.append(
                jnp.concatenate(
                    [real * cos_t + imag * sin_t, imag * cos_t - real * sin_t], axis=1
                )
            )
        yield
        spec = dot3(jnp.concatenate(turned, axis=0), ahead_ref)
        yield [
            (spec[i * blocks : (i + 1) * blocks, :rows], spec[i * blocks : (i + 1) * blocks, rows:])
            for i in range(len(signals))
        ]

    def inverse(spectra):
        parts = dot3(
            jnp.concatenate([jnp.concatenate(pair, axis=1) for pair in spectra], axis=0), back_ref
        )
        yield
        turned = []
        for i in range(len(spectra)):
            real = parts[i * blocks : (i + 1) * blocks, :rows]
            imag = parts[i * blocks : (i + 1) * blocks, rows:]
            turned.append(
                jnp.concatenate(
                    [real * cos_t - imag * sin_t, imag * cos_t + real * sin_t], axis=0
                )
            )
        yield
        high, low = split(jnp.concatenate(turned, axis=1))
        out = dot(last_ref[...], jnp.concatenate([high, high, low], axis=0))
        yield [out[:, i * rows : (i + 1) * rows] for i in range(len(spectra))]

    def starts_of(slot):
        starts = [slot // share * piece + 2 * slots + slot % share]
        for group in range(groups):
            starts += [group * piece + slot, group * piece + slots + slot]
        return starts

    def products_of(spectra):
        filt_r, filt_i = spectra[0]
        tap_r, tap_i = 0.0, 0.0
        products = []
        for group in range(groups):
            prod_r, prod_i = spectra[1 + 2 * group]
            grad_r, grad_i = spectra[2 + 2 * group]
            products.append((prod_r * filt_r - prod_i * filt_i, prod_r * filt_i + prod_i * filt_r))
            products.append((grad_r * filt_r + grad_i * filt_i, grad_i * filt_r - grad_r * filt_i))
            tap_r = tap_r + (grad_r * prod_r + grad_i * prod_i)
            tap_i = tap_i + (grad_i * prod_r - grad_r * prod_i)
        return [(tap_r, tap_i)] + products

    before = None
    for slot in range(slots + 1):
        steps = []
        if slot < slots:
            steps.append(forward([data_ref[rows_of(start), :] for start in starts_of(slot)]))
        if before is not None:
            steps.append(inverse(before))
        for _ in range(2):
            for step in steps:
                next(step)
        results = [next(step) for step in steps]
        if before is not None:
            for start, value in zip(starts_of(slot - 1), results[-1]):
                out_ref[rows_of(start), :] = value
        before = products_of(results[0]) if slot < slots else None


def gates_kernel(
    slots, query_ref, key_ref, value_ref, grad_ref, skip_ref, data_ref, dq_ref, dk_ref, dv_ref
):
    rows, channels = query_ref.shape
    devices = channels // slots
    piece = data_ref.shape[0] // devices
    per = devices // rows
    for block in range(channels // rows):
        slot, start = block // per, block % per * rows * piece
        cols = pl.ds(block * rows, rows)
        conv = data_ref[pl.ds(start + slot, rows, stride=piece), :].T
        back = data_ref[pl.ds(start + slots + slot, rows, stride=piece), :].T
        key = key_ref[:, cols].astype(f32)
        value = value_ref[:, cols].astype(f32)
        grad = grad_ref[:, cols].astype(f32)
        skip = skip_ref[:, cols]
        mixed = conv + skip * (key * value)
        product_grad = back + skip * (query_ref[:, cols].astype(f32) * grad)
        dq_ref[:, cols] = (grad * mixed).astype(bf16)
        dk_ref[:, cols] = (product_grad * value).astype(bf16)
        dv_ref[:, cols] = (product_grad * key).astype(bf16)


def own_taps_kernel(slots, devices, data_ref, *out_refs):
    rows, width = out_refs[0].shape
    piece = data_ref.shape[0] // devices
    for slot, out_ref in enumerate(out_refs):
        for block in range(width // rows):
            start = block * rows * piece + 2 * slots + slot
            out_ref[:, pl.ds(block * rows, rows)] = data_ref[pl.ds(start, rows, stride=piece), :].T


def join_kernel(share, places, fresh, grp_ref, *refs):
    blocks, out_ref, sems = refs[0 if fresh else 1 :][: len(places)], *refs[-2:]
    width = blocks[0].shape[1]
    writes = []
    for i, (flip, slot) in enumerate(places):
        start = pl.multiple_of(((grp_ref[0] ^ flip) * share + slot) * width, 128)
        writes.append(
            pltpu.make_async_copy(blocks[i], out_ref.at[:, pl.ds(start, width)], sems.at[i])
        )
    for write in writes:
        write.start()
    for write in writes:
        write.wait()


def join(grp, known, places, shape, share, begun=None):
    hbm = pl.BlockSpec(memory_space=pltpu.HBM)
    before = [] if begun is None else [begun]
    return pl.pallas_call(
        functools.partial(join_kernel, share, places, begun is None),
        out_shape=shape,
        in_specs=[pl.BlockSpec(memory_space=pltpu.SMEM)]
        + [hbm] * len(before)
        + [pl.BlockSpec(memory_space=pltpu.VMEM)] * len(places),
        out_specs=hbm,
        scratch_shapes=[pltpu.SemaphoreType.DMA((len(places),))],
        input_output_aliases={} if begun is None else {1: 0},
        compiler_params=pltpu.CompilerParams(vmem_limit_bytes=48 * 2**20),
        cost_estimate=pl.CostEstimate(flops=0, bytes_accessed=2**21, transcendentals=0),
    )(grp.reshape(1), *before, *(known[place] for place in places))


def local_call(kernel, out_shape, n_in, flops, moved, scalar=False):
    vmem = pl.BlockSpec(memory_space=pltpu.VMEM)
    specs = [pl.BlockSpec(memory_space=pltpu.SMEM)] if scalar else []
    return pl.pallas_call(
        kernel,
        out_shape=out_shape,
        in_specs=specs + [vmem] * n_in,
        out_specs=jax.tree.map(lambda _: vmem, out_shape),
        compiler_params=pltpu.CompilerParams(vmem_limit_bytes=48 * 2**20),
        cost_estimate=pl.CostEstimate(flops=flops, bytes_accessed=moved, transcendentals=0),
    )


def exchange(pieces, devices):
    flat = pieces.reshape(devices, 1, pieces.shape[0] // devices * pieces.shape[1])
    moved = lax.all_to_all(flat, ("seq", "grp"), split_axis=0, concat_axis=0, tiled=True)
    return moved.reshape(pieces.shape)


def body(query_gate, key_gate, value_in, grad_out, filter_taps, skip_gain):
    rows, channels = filter_taps.shape
    blocks, groups = lax.axis_size("seq"), lax.axis_size("grp")
    devices = blocks * groups
    slots = channels // devices
    share = slots // groups
    piece = 2 * slots + share
    width = share * devices
    grp = lax.axis_index("grp")
    gates = (query_gate[0], key_gate[0], value_in[0], grad_out[0])
    pieces = jax.ShapeDtypeStruct((devices * piece, rows), f32)
    size = devices * piece * rows * 4
    parts = 4
    sent = pl.pallas_call(
        functools.partial(pack_kernel, slots, parts),
        out_shape=pieces,
        in_specs=[pl.BlockSpec(memory_space=pltpu.SMEM)]
        + [pl.BlockSpec(memory_space=pltpu.HBM)] * 5,
        out_specs=pl.BlockSpec(memory_space=pltpu.VMEM),
        scratch_shapes=[
            pltpu.VMEM((4, rows, channels), bf16),
            pltpu.VMEM((rows, width), f32),
            pltpu.SemaphoreType.DMA((4, parts)),
            pltpu.SemaphoreType.DMA,
        ],
        compiler_params=pltpu.CompilerParams(vmem_limit_bytes=48 * 2**20),
        cost_estimate=pl.CostEstimate(flops=0, bytes_accessed=2 * size, transcendentals=0),
    )(
        grp.reshape(1),
        *(pltpu.with_memory_space_constraint(ref, pltpu.HBM) for ref in (*gates, filter_taps)),
    )
    data = exchange(sent, devices)
    tables = [
        jnp.asarray(table)
        for table in transform_tables(blocks, rows, 1.0 / math.sqrt(blocks * rows))
    ]
    result = local_call(
        functools.partial(spectral_kernel, slots, groups, blocks), pieces, 6, 5 * 10**9, 2 * size
    )(data, *tables)
    back = exchange(result, devices)
    own = local_call(
        functools.partial(own_taps_kernel, slots, devices),
        [jax.ShapeDtypeStruct((rows, devices), f32)] * share,
        1,
        0,
        rows * width * 8,
    )(back)
    flip_core, flip_chip = ([(i, i ^ step) for i in range(groups)] for step in (1, 2))
    across = [lax.ppermute(part, "grp", flip_chip) for part in own]
    beside = [lax.ppermute(part, "grp", flip_core) for part in own]
    grad_shape = jax.ShapeDtypeStruct((rows, channels), bf16)
    query_grad, key_grad, value_grad = local_call(
        functools.partial(gates_kernel, slots), [grad_shape] * 3, 6, 0, 20 * size
    )(*gates, skip_gain[None], back)
    across[0], query_grad = lax.optimization_barrier((across[0], query_grad))
    known = {}
    for slot in range(share):
        known[0, slot], known[1, slot], known[2, slot] = own[slot], beside[slot], across[slot]
    known[3, 0] = lax.ppermute(across[0], "grp", flip_core)
    filter_shape = jax.ShapeDtypeStruct((rows, channels), f32)
    early = [(flip, slot) for flip in (0, 1) for slot in range(share)] + [(2, 0)]
    begun = join(grp, known, early, filter_shape, share)
    known[2, 1], begun = lax.optimization_barrier((known[2, 1], begun))
    known[3, 1] = lax.ppermute(known[2, 1], "grp", flip_core)
    late = [(3, 0), (2, 1), (3, 1)]
    filter_grad = join(grp, known, late, filter_shape, share, begun)
    return (query_grad[None], key_grad[None], value_grad[None], filter_grad)


def solution(mesh):
    split_rows = P("grp", "seq", None)
    return jax.shard_map(
        body,
        mesh=mesh,
        in_specs=(split_rows,) * 4 + (P("seq", None), P()),
        out_specs=(split_rows,) * 3 + (P("seq", None),),
        check_vma=False,
    )
```

```python
import functools
import math

import jax
import jax.numpy as jnp
import numpy as np
from jax import lax
from jax.experimental import pallas as pl
from jax.experimental.pallas import tpu as pltpu
from jax.sharding import PartitionSpec as P

f32 = jnp.float32
bf16 = jnp.bfloat16


def halves(table):
    high = np.asarray(table, np.float32).astype(jnp.bfloat16)
    low = (table - high.astype(np.float64)).astype(np.float32).astype(jnp.bfloat16)
    return high, low


def transform_tables(blocks, rows, scale):
    full = 2 * blocks * rows
    k1 = np.arange(blocks)[:, None] + 0.5
    first = 2.0 * math.pi * k1 * np.arange(blocks)[None, :] / (2 * blocks)
    twist = 2.0 * math.pi * k1 * np.arange(rows)[None, :] / full
    last = 2.0 * math.pi * np.arange(rows)[:, None] * np.arange(rows)[None, :] / rows
    c1, s1 = np.cos(first), np.sin(first)
    c2, s2 = np.cos(last), np.sin(last)
    ahead1 = halves(np.concatenate([c1, -s1], axis=0))
    ahead2 = halves(np.block([[c2, -s2], [s2, c2]]))
    back2 = halves(np.block([[c2, s2], [-s2, c2]]))
    ahead2, back2 = (np.concatenate([h, h, l], axis=0) for h, l in (ahead2, back2))
    back1 = halves(np.concatenate([c1.T, -s1.T], axis=1) * (2.0 * scale / full))
    stack1 = np.concatenate([ahead1[0], ahead1[1], ahead1[0]], axis=1)
    unstack1 = np.concatenate([back1[0], back1[1], back1[0]], axis=1)
    turn = np.stack([np.cos(twist), np.sin(twist)]).astype(np.float32)
    return stack1, turn, ahead2, back2, unstack1


def split(value):
    high = value.astype(bf16)
    return high, (value - high.astype(f32)).astype(bf16)


def dot(left, right):
    return jnp.dot(left, right, preferred_element_type=f32)


def dot3(value, table_ref):
    high, low = split(value)
    return dot(jnp.concatenate([high, low, high], axis=1), table_ref[...])


def pack_kernel(slots, parts, grp_ref, *refs):
    sources, taps_ref, out_ref, held, taps, sems, tap_sem = refs[:4], *refs[4:]
    rows, channels = sources[0].shape
    devices = channels // slots
    share = taps.shape[1] // devices
    piece = 2 * slots + share
    per = devices // rows
    width = channels // parts
    copies = []
    for part in range(parts):
        cols = pl.ds(part * width, width)
        copies.append(
            [
                pltpu.make_async_copy(ref.at[:, cols], held.at[i, :, cols], sems.at[i, part])
                for i, ref in enumerate(sources)
            ]
        )
        for copy in copies[-1]:
            copy.start()
    start = pl.multiple_of(grp_ref[0] * taps.shape[1], 128)
    tap_copy = pltpu.make_async_copy(taps_ref.at[:, pl.ds(start, taps.shape[1])], taps, tap_sem)
    tap_copy.start()
    for block in range(channels // rows):
        if block * rows % width == 0:
            for copy in copies[block * rows // width]:
                copy.wait()
        slot, start = block // per, block % per * rows * piece
        cols = pl.ds(block * rows, rows)
        query, key, value, grad = (held[i, :, cols].astype(f32) for i in range(4))
        out_ref[pl.ds(start + slot, rows, stride=piece), :] = (key * value).T
        out_ref[pl.ds(start + slots + slot, rows, stride=piece), :] = (query * grad).T
    tap_copy.wait()
    for block in range(share * per):
        slot, start = block // per, block % per * rows * piece
        own = taps[:, pl.ds(block * rows, rows)]
        out_ref[pl.ds(start + 2 * slots + slot, rows, stride=piece), :] = own.T


def spectral_kernel(
    slots, groups, blocks, data_ref, first_ref, turn_ref, ahead_ref, back_ref, last_ref, out_ref
):
    share = slots // groups
    piece = 2 * slots + share
    rows = data_ref.shape[1]
    cos_t, sin_t = turn_ref[0], turn_ref[1]

    def rows_of(start):
        return pl.ds(start, blocks, stride=groups * piece)

    def forward(signals):
        high, low = split(jnp.concatenate(signals, axis=1))
        freq = dot(first_ref[...], jnp.concatenate([high, high, low], axis=0))
        yield
        turned = []
        for i in range(len(signals)):
            real = freq[:blocks, i * rows : (i + 1) * rows]
            imag = freq[blocks:, i * rows : (i + 1) * rows]
            turned.append(
                jnp.concatenate(
                    [real * cos_t + imag * sin_t, imag * cos_t - real * sin_t], axis=1
                )
            )
        yield
        spec = dot3(jnp.concatenate(turned, axis=0), ahead_ref)
        yield [
            (spec[i * blocks : (i + 1) * blocks, :rows], spec[i * blocks : (i + 1) * blocks, rows:])
            for i in range(len(signals))
        ]

    def inverse(spectra):
        parts = dot3(
            jnp.concatenate([jnp.concatenate(pair, axis=1) for pair in spectra], axis=0), back_ref
        )
        yield
        turned = []
        for i in range(len(spectra)):
            real = parts[i * blocks : (i + 1) * blocks, :rows]
            imag = parts[i * blocks : (i + 1) * blocks, rows:]
            turned.append(
                jnp.concatenate(
                    [real * cos_t - imag * sin_t, imag * cos_t + real * sin_t], axis=0
                )
            )
        yield
        high, low = split(jnp.concatenate(turned, axis=1))
        out = dot(last_ref[...], jnp.concatenate([high, high, low], axis=0))
        yield [out[:, i * rows : (i + 1) * rows] for i in range(len(spectra))]

    def starts_of(slot):
        starts = [slot // share * piece + 2 * slots + slot % share]
        for group in range(groups):
            starts += [group * piece + slot, group * piece + slots + slot]
        return starts

    def products_of(spectra):
        filt_r, filt_i = spectra[0]
        tap_r, tap_i = 0.0, 0.0
        products = []
        for group in range(groups):
            prod_r, prod_i = spectra[1 + 2 * group]
            grad_r, grad_i = spectra[2 + 2 * group]
            products.append((prod_r * filt_r - prod_i * filt_i, prod_r * filt_i + prod_i * filt_r))
            products.append((grad_r * filt_r + grad_i * filt_i, grad_i * filt_r - grad_r * filt_i))
            tap_r = tap_r + (grad_r * prod_r + grad_i * prod_i)
            tap_i = tap_i + (grad_i * prod_r - grad_r * prod_i)
        return [(tap_r, tap_i)] + products

    before = None
    for slot in range(slots + 1):
        steps = []
        if slot < slots:
            steps.append(forward([data_ref[rows_of(start), :] for start in starts_of(slot)]))
        if before is not None:
            steps.append(inverse(before))
        for _ in range(2):
            for step in steps:
                next(step)
        results = [next(step) for step in steps]
        if before is not None:
            for start, value in zip(starts_of(slot - 1), results[-1]):
                out_ref[rows_of(start), :] = value
        before = products_of(results[0]) if slot < slots else None


def gates_kernel(
    slots, query_ref, key_ref, value_ref, grad_ref, skip_ref, data_ref, dq_ref, dk_ref, dv_ref
):
    rows, channels = query_ref.shape
    devices = channels // slots
    piece = data_ref.shape[0] // devices
    per = devices // rows
    for block in range(channels // rows):
        slot, start = block // per, block % per * rows * piece
        cols = pl.ds(block * rows, rows)
        conv = data_ref[pl.ds(start + slot, rows, stride=piece), :].T
        back = data_ref[pl.ds(start + slots + slot, rows, stride=piece), :].T
        key = key_ref[:, cols].astype(f32)
        value = value_ref[:, cols].astype(f32)
        grad = grad_ref[:, cols].astype(f32)
        skip = skip_ref[:, cols]
        mixed = conv + skip * (key * value)
        product_grad = back + skip * (query_ref[:, cols].astype(f32) * grad)
        dq_ref[:, cols] = (grad * mixed).astype(bf16)
        dk_ref[:, cols] = (product_grad * value).astype(bf16)
        dv_ref[:, cols] = (product_grad * key).astype(bf16)


def own_taps_kernel(slots, devices, data_ref, *out_refs):
    rows, width = out_refs[0].shape
    piece = data_ref.shape[0] // devices
    for slot, out_ref in enumerate(out_refs):
        for block in range(width // rows):
            start = block * rows * piece + 2 * slots + slot
            out_ref[:, pl.ds(block * rows, rows)] = data_ref[pl.ds(start, rows, stride=piece), :].T


def join_kernel(share, places, fresh, grp_ref, *refs):
    blocks, out_ref, sems = refs[0 if fresh else 1 :][: len(places)], *refs[-2:]
    width = blocks[0].shape[1]
    writes = []
    for i, (flip, slot) in enumerate(places):
        start = pl.multiple_of(((grp_ref[0] ^ flip) * share + slot) * width, 128)
        writes.append(
            pltpu.make_async_copy(blocks[i], out_ref.at[:, pl.ds(start, width)], sems.at[i])
        )
    for write in writes:
        write.start()
    for write in writes:
        write.wait()


def join(grp, known, places, shape, share, begun=None):
    hbm = pl.BlockSpec(memory_space=pltpu.HBM)
    before = [] if begun is None else [begun]
    return pl.pallas_call(
        functools.partial(join_kernel, share, places, begun is None),
        out_shape=shape,
        in_specs=[pl.BlockSpec(memory_space=pltpu.SMEM)]
        + [hbm] * len(before)
        + [pl.BlockSpec(memory_space=pltpu.VMEM)] * len(places),
        out_specs=hbm,
        scratch_shapes=[pltpu.SemaphoreType.DMA((len(places),))],
        input_output_aliases={} if begun is None else {1: 0},
        compiler_params=pltpu.CompilerParams(vmem_limit_bytes=48 * 2**20),
        cost_estimate=pl.CostEstimate(flops=0, bytes_accessed=2**21, transcendentals=0),
    )(grp.reshape(1), *before, *(known[place] for place in places))


def local_call(kernel, out_shape, n_in, flops, moved, scalar=False):
    vmem = pl.BlockSpec(memory_space=pltpu.VMEM)
    specs = [pl.BlockSpec(memory_space=pltpu.SMEM)] if scalar else []
    return pl.pallas_call(
        kernel,
        out_shape=out_shape,
        in_specs=specs + [vmem] * n_in,
        out_specs=jax.tree.map(lambda _: vmem, out_shape),
        compiler_params=pltpu.CompilerParams(vmem_limit_bytes=48 * 2**20),
        cost_estimate=pl.CostEstimate(flops=flops, bytes_accessed=moved, transcendentals=0),
    )


def exchange(pieces, devices):
    flat = pieces.reshape(devices, 1, pieces.shape[0] // devices * pieces.shape[1])
    moved = lax.all_to_all(flat, ("seq", "grp"), split_axis=0, concat_axis=0, tiled=True)
    return moved.reshape(pieces.shape)


def body(query_gate, key_gate, value_in, grad_out, filter_taps, skip_gain):
    rows, channels = filter_taps.shape
    blocks, groups = lax.axis_size("seq"), lax.axis_size("grp")
    devices = blocks * groups
    slots = channels // devices
    share = slots // groups
    piece = 2 * slots + share
    width = share * devices
    grp = lax.axis_index("grp")
    gates = (query_gate[0], key_gate[0], value_in[0], grad_out[0])
    pieces = jax.ShapeDtypeStruct((devices * piece, rows), f32)
    size = devices * piece * rows * 4
    parts = 2
    sent = pl.pallas_call(
        functools.partial(pack_kernel, slots, parts),
        out_shape=pieces,
        in_specs=[pl.BlockSpec(memory_space=pltpu.SMEM)]
        + [pl.BlockSpec(memory_space=pltpu.HBM)] * 5,
        out_specs=pl.BlockSpec(memory_space=pltpu.VMEM),
        scratch_shapes=[
            pltpu.VMEM((4, rows, channels), bf16),
            pltpu.VMEM((rows, width), f32),
            pltpu.SemaphoreType.DMA((4, parts)),
            pltpu.SemaphoreType.DMA,
        ],
        compiler_params=pltpu.CompilerParams(vmem_limit_bytes=48 * 2**20),
        cost_estimate=pl.CostEstimate(flops=0, bytes_accessed=2 * size, transcendentals=0),
    )(
        grp.reshape(1),
        *(pltpu.with_memory_space_constraint(ref, pltpu.HBM) for ref in (*gates, filter_taps)),
    )
    data = exchange(sent, devices)
    tables = [
        jnp.asarray(table)
        for table in transform_tables(blocks, rows, 1.0 / math.sqrt(blocks * rows))
    ]
    result = local_call(
        functools.partial(spectral_kernel, slots, groups, blocks), pieces, 6, 5 * 10**9, 2 * size
    )(data, *tables)
    back = exchange(result, devices)
    own = local_call(
        functools.partial(own_taps_kernel, slots, devices),
        [jax.ShapeDtypeStruct((rows, devices), f32)] * share,
        1,
        0,
        rows * width * 8,
    )(back)
    flip_core, flip_chip = ([(i, i ^ step) for i in range(groups)] for step in (1, 2))
    across = [lax.ppermute(part, "grp", flip_chip) for part in own]
    beside = [lax.ppermute(part, "grp", flip_core) for part in own]
    grad_shape = jax.ShapeDtypeStruct((rows, channels), bf16)
    query_grad, key_grad, value_grad = local_call(
        functools.partial(gates_kernel, slots), [grad_shape] * 3, 6, 0, 20 * size
    )(*gates, skip_gain[None], back)
    across[0], query_grad = lax.optimization_barrier((across[0], query_grad))
    known = {}
    for slot in range(share):
        known[0, slot], known[1, slot], known[2, slot] = own[slot], beside[slot], across[slot]
    known[3, 0] = lax.ppermute(across[0], "grp", flip_core)
    filter_shape = jax.ShapeDtypeStruct((rows, channels), f32)
    early = [(flip, slot) for flip in (0, 1) for slot in range(share)] + [(2, 0)]
    begun = join(grp, known, early, filter_shape, share)
    known[2, 1], begun = lax.optimization_barrier((known[2, 1], begun))
    known[3, 1] = lax.ppermute(known[2, 1], "grp", flip_core)
    late = [(3, 0), (2, 1), (3, 1)]
    filter_grad = join(grp, known, late, filter_shape, share, begun)
    return (query_grad[None], key_grad[None], value_grad[None], filter_grad)


def solution(mesh):
    split_rows = P("grp", "seq", None)
    return jax.shard_map(
        body,
        mesh=mesh,
        in_specs=(split_rows,) * 4 + (P("seq", None), P()),
        out_specs=(split_rows,) * 3 + (P("seq", None),),
        check_vma=False,
    )
```
